128 devices in a mesh: dp: 16 (over x, y), mp: 8 (over z, core).
Axes of the slice: x: 4, y: 4, z: 4, core: 2. Of those that a mesh axis runs over, the one named last changes fastest.
Arguments:
- attn_heads: bfloat16 [2048, 4096], P('dp', 'mp'), may hold values from -6 to 6
- residual: bfloat16 [2048, 4096], P(('dp', 'mp')), may hold values from -24 to 24
- out_weight: bfloat16 [4096, 4096], P('mp'), may hold values from -0.09375 to 0.09375
- norm_gain: float32 [4096], replicated, may hold values from 0.5 to 1.5
- route_ids: int32 [2048, 2], P(('dp', 'mp')), may hold values from 0 to 3, all different within a row; in each aligned block of 16 rows (0 to 15, 16 to 31, ...) at most 12 rows name the same one
- route_weights: float32 [2048, 2], P(('dp', 'mp')), may hold values from 0.1 to 0.9
- gate_weights: bfloat16 [16, 3584, 4096], P('dp', 'mp'), may hold values from -0.09375 to 0.09375
- up_weights: bfloat16 [16, 3584, 4096], P('dp', 'mp'), may hold values from -0.09375 to 0.09375
- down_weights: bfloat16 [16, 3584, 4096], P('dp', 'mp'), may hold values from -0.046875 to 0.046875
Outputs:
- layer_out: bfloat16 [2048, 4096], P(('dp', 'mp'))
The draws below stay inside these ranges and needn't reach their ends.
Inputs may be any that keep to these rules, and one draw needn't show every extreme that they name: `route_ids`: each row names 2 different experts. Among the 16 rows of one device no expert is named by more than 12 rows, and in every draw some expert is named by exactly 12 rows of some device.
All inputs are finite; a program needn't handle non-finite values.
Results may differ from the reference program's by a relative error of at most 0.017.
Values may be sent and summed in bfloat16 or wider, within the bound.
A program may use at most 192 MiB of HBM per device.

```python
import math
import jax
import jax.numpy as jnp
import numpy as np
from jax import lax

D = 4096
HEADS = 32
HD = 128
FF = 14336
EXPERTS = 4
TOP = 2
TOK_DEV = 16
CAP = 12
GROUP = 4
OWNERS = 16
FF_DEV = 448
TOKENS = 2048


def draw_residual(key, part):
    key = jax.random.fold_in(key, 11)
    base = jax.random.normal(jax.random.fold_in(key, 1), (TOKENS, D), jnp.float32)
    return jnp.clip(base, -24.0, 24.0).astype(jnp.bfloat16)


def levels(key, dims, cuts, least, high):
    factor_of = 1.0
    for axis_at, blocks in cuts:
        steps = jax.random.uniform(jax.random.fold_in(jax.random.fold_in(key, 6), axis_at), (blocks,), jnp.float32, least / len(cuts), high / len(cuts))
        factor_of = factor_of * jnp.repeat(jnp.exp(steps), dims[axis_at] // blocks).reshape((-1,) + (1,) * (len(dims) - 1 - axis_at))
    return factor_of


def assign_block(stream_key, own, number, rows, count, top, reach, slope):
    order = jax.random.permutation(stream_key, count)
    crowded, common = portions_of(count, rows * top, reach, slope, True), portions_of(count, rows * top, reach, slope, False)
    places = jnp.arange(count)

    def named(sizes, turn):
        used = int((sizes > 0).sum())
        fixed = max(1, used // 4)
        shifted = fixed + (places - fixed + turn * (used - fixed)) % max(1, count - fixed)
        return jnp.zeros((count,), jnp.int32).at[order[jnp.where(places < fixed, places, shifted)]].set(jnp.asarray(sizes, jnp.int32))

    sizes = jnp.where(number % 4 == 0, named(crowded, number // 4), named(common, number - number // 4 - 1))
    mixed = jax.random.permutation(jax.random.fold_in(own, 3), count)
    donor, receiver = mixed[0:count // 2 * 2:2], mixed[1:count // 2 * 2:2]
    margin = jnp.minimum(sizes[donor] - 1, reach - sizes[receiver]) // 2
    margin = jnp.where((donor == order[0]) | (receiver == order[0]) | (sizes[receiver] == 0), 0, jnp.maximum(margin, 0))
    shifted = jax.random.randint(jax.random.fold_in(own, 4), (count // 2,), 0, 1 << 20) % (margin + 1)
    sizes = sizes.at[donor].add(-shifted).at[receiver].add(shifted)
    items = jnp.searchsorted(jnp.cumsum(sizes), jnp.arange(rows * top), side="right").astype(jnp.int32)
    listing = items.reshape(top, rows).T
    listing = listing[jax.random.permutation(jax.random.fold_in(own, 1), rows)]
    turn = jax.random.randint(jax.random.fold_in(own, 2), (rows, 1), 0, top)
    return jnp.take_along_axis(listing, (jnp.arange(top)[None, :] + turn) % top, axis=1)


def portions_of(amount, total, limit, slope, full):
    weights = [(1 << 20) // math.isqrt(grade ** slope) + 1 for grade in range(1, amount + 1)]
    largest = limit if full else min(limit, max(-(-total // amount), total * weights[0] // sum(weights)))
    least = 1 if total - largest >= amount - 1 else 0
    given, surplus = [largest] + [least] * (amount - 1), total - largest - least * (amount - 1)
    while surplus > 0:
        movable = [i for i in range(1, amount) if given[i] < largest] or [i for i in range(1, amount) if given[i] < limit]
        pool, budget = sum([weights[i] for i in movable]), surplus
        for i in movable:
            more = min(limit - given[i], max(1, budget * weights[i] // pool), surplus)
            given[i] = given[i] + more
            surplus = surplus - more
    return np.array(given)


def noise(key, shape, spread, most, cuts=(), kind=jnp.bfloat16):
    entries = jax.random.normal(key, shape, jnp.float32) * spread
    if len(cuts) > 0:
        entries = levels(key, shape, cuts, -0.22, 0.18) * entries
    return jnp.clip(entries, min=-most, max=most).astype(kind)


def setup_inputs(seed: int = 0) -> dict:
    key_list = jax.random.split(jax.random.key(seed), 10)
    attn_heads = noise(key_list[0], (TOKENS, HEADS * HD), 1.0, 6.0, ((0, 16), (1, 8)))
    residual = draw_residual(jax.random.fold_in(key_list[9], 71), 0)
    out_weight = noise(key_list[2], (HEADS * HD, D), (HEADS * HD) ** -0.5, 0.09375, ((0, 8),))
    norm_gain = jnp.clip(1.0 + 0.1 * jax.random.normal(key_list[3], (D,), jnp.float32), 0.5, 1.5)
    route_ids_keys = jax.random.split(jax.random.fold_in(key_list[4], 1), TOKENS // TOK_DEV)
    route_ids_turns = jax.random.permutation(jax.random.fold_in(key_list[4], 3), TOKENS // TOK_DEV)
    route_ids = jax.vmap(lambda own, number: assign_block(jax.random.fold_in(key_list[4], 2), own, number, TOK_DEV, EXPERTS, TOP, CAP, 2))(route_ids_keys, route_ids_turns).reshape((TOKENS, TOP))
    route_weights = jnp.clip(0.1 + 0.79999997 * jax.random.uniform(key_list[5], (TOKENS, TOP), jnp.float32) ** levels(key_list[5], (TOKENS, TOP), ((0, 128),), -0.2, 0.2), 0.1, 0.9)
    gate_weights = noise(key_list[6], (OWNERS, FF // GROUP, D), D ** -0.5, 0.09375, ((0, 16), (1, 8)))
    up_weights = noise(key_list[7], (OWNERS, FF // GROUP, D), D ** -0.5, 0.09375, ((0, 16), (1, 8)))
    down_weights = noise(key_list[8], (OWNERS, FF // GROUP, D), FF ** -0.5, 0.046875, ((0, 16), (1, 8)))
    return {"attn_heads": attn_heads, "residual": residual, "out_weight": out_weight, "norm_gain": norm_gain, "route_ids": route_ids, "route_weights": route_weights, "gate_weights": gate_weights, "up_weights": up_weights, "down_weights": down_weights}


def expert_output(normed, gate_rows, up_rows, down_rows):
    gate = lax.dot_general(normed, gate_rows, (((1,), (1,)), ((), ())), preferred_element_type=jnp.float32)
    up = lax.dot_general(normed, up_rows, (((1,), (1,)), ((), ())), preferred_element_type=jnp.float32)
    act = (jax.nn.silu(gate) * up).astype(jnp.bfloat16)

    def add_block(index, total):
        start = (index * FF_DEV).astype(jnp.int32)
        left = lax.dynamic_slice_in_dim(act, start, FF_DEV, 1)
        right = lax.dynamic_slice_in_dim(down_rows, start, FF_DEV, 0)
        piece = jnp.dot(left, right, preferred_element_type=jnp.float32).astype(jnp.bfloat16)
        piece = lax.optimization_barrier(piece)
        return total + piece.astype(jnp.float32)
    empty = jnp.zeros((normed.shape[0], D), jnp.float32)
    return lax.fori_loop(jnp.int32(0), jnp.int32(FF // FF_DEV), add_block, empty)

def reference(attn_heads, residual, out_weight, norm_gain, route_ids, route_weights, gate_weights, up_weights, down_weights):
    proj = jnp.dot(attn_heads, out_weight, preferred_element_type=jnp.float32)
    hidden = residual.astype(jnp.float32) + proj
    square = lax.optimization_barrier(jnp.mean(hidden * hidden, axis=1, keepdims=True))
    normed = (hidden * lax.rsqrt(square + 1e-05) * norm_gain.astype(jnp.float32)).astype(jnp.bfloat16)
    moe = jnp.zeros((TOKENS, D), jnp.float32)
    for expert in range(EXPERTS):
        weight = lax.optimization_barrier(jnp.sum(jnp.where(route_ids == expert, route_weights, jnp.float32(0.0)), axis=1))
        gate_rows = gate_weights[expert * GROUP:(expert + 1) * GROUP].reshape(FF, D)
        up_rows = up_weights[expert * GROUP:(expert + 1) * GROUP].reshape(FF, D)
        down_rows = down_weights[expert * GROUP:(expert + 1) * GROUP].reshape(FF, D)
        moe = moe + weight[:, None] * expert_output(normed, gate_rows, up_rows, down_rows)
    return (hidden + moe).astype(jnp.bfloat16)
```

```python
import jax
import jax.numpy as jnp
from jax import lax
from jax.experimental import pallas as pl
from jax.experimental.pallas import tpu as pltpu
from jax.sharding import PartitionSpec as P

MESH = pl.DeviceIdType.MESH
BF = jnp.bfloat16
F32 = jnp.float32
D = 4096
CAP = 12
TOK = 16
FF = 448
BLK = 48
QUAD = 4 * BLK
GRP = 2 * QUAD
HALF = D // 2
NCH = 4
CH = D // NCH
LO = pl.ds(0, HALF)
HI = pl.ds(HALF, HALF)
NT = (((1,), (1,)), ((), ()))


def mod4(v):
    return lax.rem(v, 4)


def kernel(
    attn, resid, ow_h, gain, ids, rw, g_h, u_h, d_h, out,
    ow, wg, wu, wd, pbuf, sibp, psum, zr, hid, meta, selw, nb,
    tok, part, drecv, fq, nl, nr, fp, nlp, nrp, acc_g, acc_u, act, back, xr,
    wsem, ps_s, ps_r, z_s, z_r, m_s, m_r, x_s, x_r, a_s, a_r, b_s, b_r,
    d_s, d_r, e_s, e_r, q_s, q_r, p_s, p_r, o_s, o_r,
):
    dp = lax.axis_index("dp")
    mp = lax.axis_index("mp")
    x, y = lax.div(dp, 4), lax.rem(dp, 4)
    z, c = lax.div(mp, 2), lax.rem(mp, 2)
    o = 1 - c
    p = y * o + z * c
    q = z * o + y * c

    def at_p(k):
        t = mod4(p + k)
        return (x * 4 + t * o + q * c, (q * o + t * c) * 2 + c)

    def at_q(k):
        t = mod4(q + k)
        return (x * 4 + p * o + t * c, (t * o + p * c) * 2 + c)

    def at_x(k):
        return (mod4(x + k) * 4 + y, mp)

    def at_z(k):
        return (dp, mod4(z + k) * 2 + c)

    def at_y(k):
        return (x * 4 + mod4(y + k), mp)

    sib = (dp, z * 2 + o)
    sent = []

    def remote(src, dst, ss, rs, dev):
        return pltpu.make_async_remote_copy(
            src_ref=src, dst_ref=dst, send_sem=ss, recv_sem=rs, device_id=dev, device_id_type=MESH
        )

    def go(copy):
        copy.start()
        sent.append(copy)
        return copy

    def cols(k):
        return pl.ds(k * CH, CH)

    loads = [pltpu.make_async_copy(ow_h.at[:, cols(k)], ow.at[:, cols(k)], wsem.at[k]) for k in range(NCH)]
    experts = [
        pltpu.make_async_copy(g_h.at[0], wg, wsem.at[NCH]),
        pltpu.make_async_copy(u_h.at[0], wu, wsem.at[NCH + 1]),
        pltpu.make_async_copy(d_h.at[0], wd, wsem.at[NCH + 2]),
    ]
    for cp in loads:
        cp.start()

    lane = lax.broadcasted_iota(jnp.int32, (TOK, 128), 1)
    i_f = ids[...].astype(F32)
    w_f = rw[...]
    meta[pl.ds(0, TOK), :] = jnp.where(
        lane == 0, i_f[:, 0:1],
        jnp.where(lane == 1, i_f[:, 1:2], jnp.where(lane == 2, w_f[:, 0:1], jnp.where(lane == 3, w_f[:, 1:2], 0.0))),
    )
    meta[pl.ds(64, 64), :] = jnp.zeros((64, 128), F32)

    barrier = pltpu.get_barrier_semaphore()
    greet = [sib, at_x(1), at_x(2), at_x(3), at_z(1), at_z(2), at_z(3), at_y(1), at_y(3)]
    for dev in greet:
        pl.semaphore_signal(barrier, inc=1, device_id=dev, device_id_type=MESH)
    pl.semaphore_wait(barrier, len(greet))

    metas = [
        go(remote(meta.at[pl.ds(0, TOK)], meta.at[pl.ds((4 - k) * TOK, TOK)], m_s.at[k - 1], m_r.at[k - 1], at_x(k)))
        for k in (1, 2, 3)
    ]

    sibs = []
    for k in range(NCH):
        loads[k].wait()
        pr = jnp.dot(attn[...], ow[:, cols(k)], preferred_element_type=F32)
        pbuf[:, :, :, cols(k)] = pr.astype(BF).reshape(4, 2, TOK, CH)
        sibs.append(go(remote(pbuf.at[:, o, :, cols(k)], sibp.at[:, :, cols(k)], ps_s.at[k], ps_r.at[k], sib)))
    for cp in experts:
        cp.start()
    zs = []
    for k in range(NCH):
        sibs[k].wait_recv()
        psum[:, :, cols(k)] = (pbuf[:, c, :, cols(k)].astype(F32) + sibp[:, :, cols(k)].astype(F32)).astype(BF)
        zs.append([
            go(remote(psum.at[mod4(z + j), :, cols(k)], zr.at[j - 1, :, cols(k)], z_s.at[k, j - 1], z_r.at[k, j - 1], at_z(j)))
            for j in (1, 2, 3)
        ])
    square = jnp.zeros((TOK, 1), F32)
    for k in range(NCH):
        for cp in zs[k]:
            cp.wait_recv()
        h = resid[:, cols(k)].astype(F32) + psum[z, :, cols(k)].astype(F32)
        for j in range(3):
            h = h + zr[j, :, cols(k)].astype(F32)
        hid[:, cols(k)] = h
        square = square + jnp.sum(h * h, axis=1, keepdims=True)
    scale = lax.rsqrt(square * (1.0 / D) + 1e-05)
    xs = []
    for k in range(NCH):
        nb[pl.ds(0, TOK), cols(k)] = (hid[:, cols(k)] * scale * gain[:, cols(k)]).astype(BF)
        xs.append([
            go(remote(nb.at[pl.ds(0, TOK), cols(k)], nb.at[pl.ds((4 - j) * TOK, TOK), cols(k)], x_s.at[k, j - 1], x_r.at[k, j - 1], at_x(j)))
            for j in (1, 2, 3)
        ])

    for cp in metas:
        cp.wait_recv()
    tr = meta[...].T
    xf = x.astype(F32)
    col = lax.broadcasted_iota(jnp.int32, (8, 128), 1)
    in0 = jnp.logical_and(tr[0:1, :] == xf, col[0:1] < 64)
    in1 = jnp.logical_and(tr[1:2, :] == xf, col[0:1] < 64)
    uses = jnp.where(jnp.logical_or(in0, in1), 1.0, 0.0).astype(F32)
    weight = jnp.where(in0, tr[2:3, :], 0.0) + jnp.where(in1, tr[3:4, :], 0.0)
    ra = lax.broadcasted_iota(jnp.int32, (128, 128), 0)
    rb = lax.broadcasted_iota(jnp.int32, (128, 128), 1)
    earlier = jnp.where(jnp.logical_and(lax.div(ra, TOK) == lax.div(rb, TOK), ra < rb), 1.0, 0.0).astype(F32)
    rank = jnp.dot(jnp.broadcast_to(uses, (8, 128)), earlier, preferred_element_type=F32)
    slot = rank + (lax.div(col, TOK) * CAP).astype(F32)
    rows = lax.broadcasted_iota(jnp.int32, (BLK, 128), 0).astype(F32)
    hit = jnp.logical_and(rows == slot[0:1, :], uses > 0.5)
    sel = jnp.where(hit, 1.0, 0.0).astype(BF)[:, 0:64]
    selw[...] = jnp.where(hit, weight, 0.0)

    def blk(g, color, r):
        return tok.at[g, pl.ds(color * QUAD + r * BLK, BLK)]

    HV = (LO, HI)

    def near_p(h):
        s = blk(0, 0, 0).at[:, HV[h]]
        return [
            go(remote(s, blk(3, 0, 0).at[:, HV[h]], a_s.at[h], a_r.at[h], at_p(1))),
            go(remote(s, blk(1, 0, 0).at[:, HV[h]], a_s.at[2 + h], a_r.at[2 + h], at_p(3))),
        ]

    def near_q(g, h):
        s = blk(g, 0, 0).at[:, HV[h]]
        return [
            go(remote(s, blk(g, 0, 3).at[:, HV[h]], b_s.at[g, h], b_r.at[g, h], at_q(1))),
            go(remote(s, blk(g, 0, 1).at[:, HV[h]], b_s.at[g, 2 + h], b_r.at[g, 2 + h], at_q(3))),
        ]

    def share(g, r):
        return go(remote(blk(g, 0, r), blk(g, 1, r), d_s.at[g, r], d_r.at[g, r], sib))

    pn, qn, shared, qf = [None] * 2, [[None, None] for _ in range(4)], {}, [None] * 4
    for h in range(2):
        for k in (2 * h, 2 * h + 1):
            for cp in xs[k]:
                cp.wait_recv()
            tok[0, pl.ds(0, BLK), cols(k)] = jnp.dot(sel, nb[:, cols(k)], preferred_element_type=F32).astype(BF)
        pn[h] = near_p(h)
        qn[0][h] = near_q(0, h)
    shared[0, 0] = share(0, 0)

    def relay_q(g):
        qn[g][0][0].wait_recv()
        lo = go(remote(blk(g, 0, 3).at[:, LO], blk(g, 0, 2).at[:, LO], b_s.at[g, 4], b_r.at[g, 4], at_q(1)))
        qn[g][1][1].wait_recv()
        hi = go(remote(blk(g, 0, 1).at[:, HI], blk(g, 0, 2).at[:, HI], b_s.at[g, 5], b_r.at[g, 5], at_q(3)))
        qf[g] = (lo, hi)
        qn[g][1][0].wait_recv()
        shared[g, 3] = share(g, 3)
        qn[g][0][1].wait_recv()
        shared[g, 1] = share(g, 1)

    def far_q(g):
        qf[g][0].wait_recv()
        qf[g][1].wait_recv()
        shared[g, 2] = share(g, 2)

    def begin(g):
        for h in range(2):
            qn[g][h] = near_q(g, h)
        shared[g, 0] = share(g, 0)

    def compute(g):
        for r in (0, 3, 1, 2):
            shared[g, r].wait_recv()
        for k in range(2):
            ks = pl.ds(k * HALF, HALF)
            rows_in = tok[g, :, ks]
            gate = lax.dot_general(rows_in, wg[:, ks], NT, preferred_element_type=F32)
            if k == 0:
                acc_g[...] = gate
            else:
                acc_g[...] += gate
            up = lax.dot_general(rows_in, wu[:, ks], NT, preferred_element_type=F32)
            if k == 0:
                acc_u[...] = up
            else:
                acc_u[...] += up
        gate = acc_g[...]
        act[...] = (gate / (1.0 + jnp.exp(-gate)) * acc_u[...]).astype(BF)
        for k in range(4):
            ks = cols(k)
            part[g, :, ks] = jnp.dot(act[...], wd[:, ks], preferred_element_type=F32).astype(BF)
        return go(remote(part.at[g, pl.ds(QUAD, QUAD)], drecv.at[g], e_s.at[g], e_r.at[g], sib))

    def add(dst, srcs, at, width):
        def step(i, carry):
            ks = pl.ds(pl.multiple_of(at + i * 512, 512), 512)
            total = dst[:, ks].astype(F32)
            for s in srcs:
                total = total + s[:, ks].astype(F32)
            dst[:, ks] = total.astype(BF)
            return carry

        lax.fori_loop(0, width // 512, step, 0)

    def prt(g, r):
        return part.at[g, pl.ds(r * BLK, BLK)]

    def back_q1(g, esend):
        esend.wait_recv()
        add(part.at[g, pl.ds(0, QUAD)], [drecv.at[g]], 0, D)
        f_lo = go(remote(prt(g, 2).at[:, LO], fq.at[g, :, LO], q_s.at[g, 0], q_r.at[g, 0], at_q(1)))
        f_hi = go(remote(prt(g, 2).at[:, HI], fq.at[g, :, HI], q_s.at[g, 1], q_r.at[g, 1], at_q(3)))
        n1 = go(remote(prt(g, 1).at[:, HI], nl.at[g, :, HI], q_s.at[g, 2], q_r.at[g, 2], at_q(1)))
        n3 = go(remote(prt(g, 3).at[:, LO], nr.at[g, :, LO], q_s.at[g, 3], q_r.at[g, 3], at_q(3)))
        return [f_lo, f_hi, n1, n3]

    def back_q2(g, st):
        st[0].wait_recv()
        add(prt(g, 1), [fq.at[g]], 0, HALF)
        n1 = go(remote(prt(g, 1).at[:, LO], nl.at[g, :, LO], q_s.at[g, 4], q_r.at[g, 4], at_q(1)))
        st[1].wait_recv()
        add(prt(g, 3), [fq.at[g]], HALF, HALF)
        n3 = go(remote(prt(g, 3).at[:, HI], nr.at[g, :, HI], q_s.at[g, 5], q_r.at[g, 5], at_q(3)))
        st += [n1, n3]

    def back_q3(g, st):
        for cp in st[2:]:
            cp.wait_recv()
        add(prt(g, 0), [nl.at[g], nr.at[g]], 0, D)

    relay_q(0)
    pn[0][0].wait_recv()
    pf_lo = go(remote(blk(3, 0, 0).at[:, LO], blk(2, 0, 0).at[:, LO], a_s.at[4], a_r.at[4], at_p(1)))
    pn[1][1].wait_recv()
    pf_hi = go(remote(blk(1, 0, 0).at[:, HI], blk(2, 0, 0).at[:, HI], a_s.at[5], a_r.at[5], at_p(3)))
    pn[1][0].wait_recv()
    begin(3)
    pn[0][1].wait_recv()
    begin(1)
    far_q(0)
    pf_lo.wait_recv()
    pf_hi.wait_recv()
    begin(2)
    for cp in experts:
        cp.wait()
    e0 = compute(0)
    relay_q(3)
    relay_q(1)
    far_q(3)
    e3 = compute(3)
    relay_q(2)
    far_q(1)
    r0 = back_q1(0, e0)
    e1 = compute(1)
    far_q(2)
    back_q2(0, r0)
    r3 = back_q1(3, e3)
    e2 = compute(2)
    r1 = back_q1(1, e1)
    back_q2(3, r3)
    r2 = back_q1(2, e2)
    back_q2(1, r1)
    back_q2(2, r2)
    back_q3(2, r2)
    far_lo = go(remote(prt(2, 0).at[:, LO], fp.at[:, LO], p_s.at[0], p_r.at[0], at_p(1)))
    far_hi = go(remote(prt(2, 0).at[:, HI], fp.at[:, HI], p_s.at[1], p_r.at[1], at_p(3)))
    back_q3(1, r1)
    t1 = go(remote(prt(1, 0).at[:, HI], nlp.at[:, HI], p_s.at[2], p_r.at[2], at_p(1)))
    back_q3(3, r3)
    t3 = go(remote(prt(3, 0).at[:, LO], nrp.at[:, LO], p_s.at[3], p_r.at[3], at_p(3)))
    back_q3(0, r0)
    far_lo.wait_recv()
    add(prt(1, 0), [fp], 0, HALF)
    t1b = go(remote(prt(1, 0).at[:, LO], nlp.at[:, LO], p_s.at[4], p_r.at[4], at_p(1)))
    far_hi.wait_recv()
    add(prt(3, 0), [fp], HALF, HALF)
    t3b = go(remote(prt(3, 0).at[:, HI], nrp.at[:, HI], p_s.at[5], p_r.at[5], at_p(3)))
    for cp in (t1, t3, t1b, t3b):
        cp.wait_recv()

    ws = selw[:, 0:64]
    os_ = []
    for k in range(NCH):
        ks = cols(k)
        total = prt(0, 0)[:, ks].astype(F32) + nlp[:, ks].astype(F32) + nrp[:, ks].astype(F32)
        back[:, ks] = lax.dot_general(
            ws, total, (((0,), (0,)), ((), ())), precision=lax.Precision.HIGHEST, preferred_element_type=F32
        ).astype(BF)
        os_.append([
            go(remote(back.at[pl.ds(j * TOK, TOK), ks], xr.at[j - 1, :, ks], o_s.at[k, j - 1], o_r.at[k, j - 1], at_x(j)))
            for j in (1, 2, 3)
        ])
    for k in range(NCH):
        ks = cols(k)
        for cp in os_[k]:
            cp.wait_recv()
        total = hid[:, ks] + back[pl.ds(0, TOK), ks].astype(F32)
        for j in range(3):
            total = total + xr[j, :, ks].astype(F32)
        out[:, ks] = total.astype(BF)
    for cp in sent:
        cp.wait_send()


def body(attn_heads, residual, out_weight, norm_gain, route_ids, route_weights, gate_weights, up_weights, down_weights):
    vmem = pl.BlockSpec(memory_space=pltpu.VMEM)
    hbm = pl.BlockSpec(memory_space=pl.ANY)
    dma = pltpu.SemaphoreType.DMA
    V = pltpu.VMEM
    return pl.pallas_call(
        kernel,
        out_shape=jax.ShapeDtypeStruct((TOK, D), BF),
        in_specs=[vmem, vmem, hbm, vmem, vmem, vmem, hbm, hbm, hbm],
        out_specs=vmem,
        scratch_shapes=[
            V((512, D), BF), V((FF, D), BF), V((FF, D), BF), V((FF, D), BF),
            V((4, 2, TOK, D), BF), V((4, TOK, D), BF), V((4, TOK, D), BF), V((3, TOK, D), BF),
            V((TOK, D), F32), V((128, 128), F32), V((BLK, 128), F32), V((4 * TOK, D), BF),
            V((4, GRP, D), BF), V((4, GRP, D), BF), V((4, QUAD, D), BF),
            V((4, BLK, D), BF), V((4, BLK, D), BF), V((4, BLK, D), BF),
            V((BLK, D), BF), V((BLK, D), BF), V((BLK, D), BF),
            V((GRP, FF), F32), V((GRP, FF), F32), V((GRP, FF), BF),
            V((4 * TOK, D), BF), V((3, TOK, D), BF),
            dma((NCH + 3,)),
            dma((NCH,)), dma((NCH,)), dma((NCH, 3)), dma((NCH, 3)),
            dma((3,)), dma((3,)), dma((NCH, 3)), dma((NCH, 3)),
            dma((6,)), dma((6,)), dma((4, 6)), dma((4, 6)),
            dma((4, 4)), dma((4, 4)), dma((4,)), dma((4,)),
            dma((4, 6)), dma((4, 6)), dma((6,)), dma((6,)),
            dma((NCH, 3)), dma((NCH, 3)),
        ],
        compiler_params=pltpu.CompilerParams(
            collective_id=0, has_side_effects=True, vmem_limit_bytes=60 * 2**20
        ),
    )(attn_heads, residual, out_weight, norm_gain.reshape(1, D), route_ids, route_weights, gate_weights, up_weights, down_weights)


def solution(mesh):
    placed = (
        P("dp", "mp"),
        P(("dp", "mp"), None),
        P("mp", None),
        P(),
        P(("dp", "mp"), None),
        P(("dp", "mp"), None),
        P("dp", "mp", None),
        P("dp", "mp", None),
        P("dp", "mp", None),
    )
    return jax.shard_map(
        body, mesh=mesh, in_specs=placed, out_specs=P(("dp", "mp"), None), check_vma=False
    )
```

```python
import jax
import jax.numpy as jnp
from jax import lax
from jax.experimental import pallas as pl
from jax.experimental.pallas import tpu as pltpu
from jax.sharding import PartitionSpec as P

MESH = pl.DeviceIdType.MESH
BF = jnp.bfloat16
F32 = jnp.float32
D = 4096
CAP = 12
TOK = 16
FF = 448
BLK = 48
QUAD = 4 * BLK
GRP = 2 * QUAD
HALF = D // 2
NCH = 4
CH = D // NCH
EXT = 128
WID = EXT + D + EXT
LO = pl.ds(0, HALF)
HI = pl.ds(HALF, HALF)
HX = pl.ds(HALF, HALF + EXT)
NT = (((1,), (1,)), ((), ()))


def mod4(v):
    return lax.rem(v, 4)


def kernel(
    attn, resid, ow_h, gain, ids, rw, g_h, u_h, d_h, out,
    ow, wg, wu, wd, pbuf, sibp, zr, hid, turn, selw, onehot, nb,
    tok, part, drecv, fq, nl, nr, acc_g, acc_u, act, xr, yr,
    wsem, ps_s, ps_r, z_s, z_r, x_s, x_r, a_s, a_r, b_s, b_r,
    d_s, d_r, e_s, e_r, q_s, q_r, p_s, p_r, o_s, o_r,
):
    dp = lax.axis_index("dp")
    mp = lax.axis_index("mp")
    x, y = lax.div(dp, 4), lax.rem(dp, 4)
    z, c = lax.div(mp, 2), lax.rem(mp, 2)
    o = 1 - c
    p = y * o + z * c
    q = z * o + y * c

    def at_p(k):
        t = mod4(p + k)
        return (x * 4 + t * o + q * c, (q * o + t * c) * 2 + c)

    def at_q(k):
        t = mod4(q + k)
        return (x * 4 + p * o + t * c, (t * o + p * c) * 2 + c)

    def at_x(k):
        return (mod4(x + k) * 4 + y, mp)

    def at_z(k):
        return (dp, mod4(z + k) * 2 + c)

    def at_y(k):
        return (x * 4 + mod4(y + k), mp)

    sib = (dp, z * 2 + o)
    sent = []

    def remote(src, dst, ss, rs, dev):
        return pltpu.make_async_remote_copy(
            src_ref=src, dst_ref=dst, send_sem=ss, recv_sem=rs, device_id=dev, device_id_type=MESH
        )

    def go(copy):
        copy.start()
        sent.append(copy)
        return copy

    def cols(k):
        return pl.ds(k * CH, CH)

    loads = [pltpu.make_async_copy(ow_h.at[:, cols(k)], ow.at[:, cols(k)], wsem.at[k]) for k in range(NCH)]
    experts = [
        pltpu.make_async_copy(g_h.at[0], wg, wsem.at[NCH]),
        pltpu.make_async_copy(u_h.at[0], wu, wsem.at[NCH + 1]),
        pltpu.make_async_copy(d_h.at[0], wd, wsem.at[NCH + 2]),
    ]
    for cp in loads:
        cp.start()

    def terms(v):
        first = v.astype(BF).astype(F32)
        second = (v - first).astype(BF).astype(F32)
        return first, second, v - first - second

    turn[...] = jnp.zeros((128, 128), F32)
    turn[0:2, 0:TOK] = ids[...].astype(F32)
    for n, v in enumerate(terms(rw[...])):
        turn[2 + 2 * n : 4 + 2 * n, 0:TOK] = v
    nb[0, pl.ds(0, TOK), pl.ds(0, EXT)] = turn[...].T[0:TOK].astype(BF)
    turn[...] = jnp.zeros((128, 128), F32)

    barrier = pltpu.get_barrier_semaphore()
    greet = [sib, at_x(1), at_x(2), at_x(3), at_z(1), at_z(2), at_z(3), at_y(1), at_y(2), at_y(3)]
    for dev in greet:
        pl.semaphore_signal(barrier, inc=1, device_id=dev, device_id_type=MESH)
    for k in range(NCH):
        loads[k].wait()
        pr = jnp.dot(attn[...], ow[:, cols(k)], preferred_element_type=F32)
        pbuf[:, :, :, cols(k)] = pr.astype(BF).reshape(4, 2, TOK, CH)
    pl.semaphore_wait(barrier, len(greet))

    sibs = [
        go(remote(pbuf.at[:, o, :, cols(k)], sibp.at[:, :, cols(k)], ps_s.at[k], ps_r.at[k], sib)) for k in range(NCH)
    ]
    zs = []
    for k in range(NCH):
        sibs[k].wait_recv()
        sibp[:, :, cols(k)] = (pbuf[:, c, :, cols(k)].astype(F32) + sibp[:, :, cols(k)].astype(F32)).astype(BF)
        zs.append([
            go(remote(sibp.at[mod4(z + j), :, cols(k)], zr.at[j - 1, :, cols(k)], z_s.at[k, j - 1], z_r.at[k, j - 1], at_z(j)))
            for j in (1, 2, 3)
        ])
    def at(k):
        return pl.ds(k * CH + (EXT if k else 0), CH + (EXT if k in (0, NCH - 1) else 0))

    def body_of(k):
        return pl.ds(EXT + k * CH, CH)

    square, xs, ps = [], {}, {}

    def along_x(g, k, span):
        xs[g, k] = [
            go(remote(nb.at[g, pl.ds(0, TOK), span], nb.at[g, pl.ds((4 - j) * TOK, TOK), span], x_s.at[g, k, j - 1], x_r.at[g, k, j - 1], at_x(j)))
            for j in (1, 2, 3)
        ]

    def along_p(k):
        ps[k] = [
            go(remote(nb.at[0, pl.ds(0, TOK), at(k)], nb.at[4 - j, pl.ds(0, TOK), at(k)], a_s.at[k, j - 1], a_r.at[k, j - 1], at_p(j)))
            for j in (1, 2, 3)
        ]

    def hidden(k):
        for cp in zs[k]:
            cp.wait_recv()
        h = resid[:, cols(k)].astype(F32) + sibp[z, :, cols(k)].astype(F32)
        for j in range(3):
            h = h + zr[j, :, cols(k)].astype(F32)
        hid[:, cols(k)] = h
        square.append(jnp.sum(h * h, axis=1, keepdims=True))
        nb[0, pl.ds(0, TOK), body_of(k)] = (h * gain[:, cols(k)]).astype(BF)
        if k == NCH - 1:
            first, second, third = terms(lax.rsqrt((square[0] + square[1] + square[2] + square[3]) * (1.0 / D) + 1e-05))
            lane = lax.broadcasted_iota(jnp.int32, (TOK, EXT), 1)
            nb[0, pl.ds(0, TOK), pl.ds(EXT + D, EXT)] = jnp.where(
                lane == 0, first, jnp.where(lane == 1, second, jnp.where(lane == 2, third, 0.0))
            ).astype(BF)
        along_x(0, k, at(k))
        along_p(k)

    xf = x.astype(F32)

    def routes(g):
        turn[0 : 4 * TOK, :] = nb[g, :, pl.ds(0, EXT)].astype(F32)
        tr = turn[...].T
        col = lax.broadcasted_iota(jnp.int32, (8, 128), 1)
        in0 = jnp.logical_and(tr[0:1, :] == xf, col[0:1] < 64)
        in1 = jnp.logical_and(tr[1:2, :] == xf, col[0:1] < 64)
        uses = jnp.where(jnp.logical_or(in0, in1), 1.0, 0.0).astype(F32)
        w0 = tr[2:3, :] + tr[4:5, :] + tr[6:7, :]
        w1 = tr[3:4, :] + tr[5:6, :] + tr[7:8, :]
        weight = jnp.where(in0, w0, 0.0) + jnp.where(in1, w1, 0.0)
        ra = lax.broadcasted_iota(jnp.int32, (128, 128), 0)
        rb = lax.broadcasted_iota(jnp.int32, (128, 128), 1)
        earlier = jnp.where(jnp.logical_and(lax.div(ra, TOK) == lax.div(rb, TOK), ra < rb), 1.0, 0.0).astype(F32)
        rank = jnp.dot(jnp.broadcast_to(uses, (8, 128)), earlier, preferred_element_type=F32)
        slot = rank + (lax.div(col, TOK) * CAP).astype(F32)
        rows = lax.broadcasted_iota(jnp.int32, (BLK, 128), 0).astype(F32)
        hit = jnp.logical_and(rows == slot[0:1, :], uses > 0.5)
        selw[g] = jnp.where(hit, weight, 0.0)
        onehot[g] = jnp.where(hit, 1.0, 0.0)
        return jnp.where(hit, 1.0, 0.0).astype(BF)[:, 0:64]

    def pick(g, sel, start, width):
        tok[g, pl.ds(0, BLK), pl.ds(start, width)] = jnp.dot(
            sel, nb[g, :, pl.ds(EXT + start, width)], preferred_element_type=F32
        ).astype(BF)

    def blk(g, color, r):
        return tok.at[g, pl.ds(color * QUAD + r * BLK, BLK)]

    HV = (LO, HX)
    NV = (pl.ds(0, EXT + HALF), pl.ds(EXT + HALF, HALF + EXT))

    def near_q(g, h):
        s = blk(g, 0, 0).at[:, HV[h]]
        return [
            go(remote(s, blk(g, 0, 3).at[:, HV[h]], b_s.at[g, h], b_r.at[g, h], at_q(1))),
            go(remote(s, blk(g, 0, 1).at[:, HV[h]], b_s.at[g, 2 + h], b_r.at[g, 2 + h], at_q(3))),
        ]

    def share(g, r):
        return go(remote(blk(g, 0, r), blk(g, 1, r), d_s.at[g, r], d_r.at[g, r], sib))

    qn, shared, qf = [[None, None] for _ in range(4)], {}, [None] * 4

    def relay_q(g):
        qn[g][0][0].wait_recv()
        lo = go(remote(blk(g, 0, 3).at[:, LO], blk(g, 0, 2).at[:, LO], b_s.at[g, 4], b_r.at[g, 4], at_q(1)))
        qn[g][1][1].wait_recv()
        hi = go(remote(blk(g, 0, 1).at[:, HX], blk(g, 0, 2).at[:, HX], b_s.at[g, 5], b_r.at[g, 5], at_q(3)))
        qf[g] = (lo, hi)
        qn[g][1][0].wait_recv()
        shared[g, 3] = share(g, 3)
        qn[g][0][1].wait_recv()
        shared[g, 1] = share(g, 1)

    def far_q(g):
        qf[g][0].wait_recv()
        qf[g][1].wait_recv()
        shared[g, 2] = share(g, 2)

    def begin(g, h):
        qn[g][h] = near_q(g, h)
        if h == 1:
            shared[g, 0] = share(g, 0)

    def pass_on(h):
        for g in (3, 1, 2):
            for k in (2 * h, 2 * h + 1):
                ps[k][3 - g].wait_recv()
            along_x(g, h, NV[h])

    def enter(g):
        for h in range(2):
            for cp in xs[g, h]:
                cp.wait_recv()
            if h == 0:
                sel = routes(g)
                pick(g, sel, 0, HALF)
            else:
                pick(g, sel, HALF, HALF + EXT)
            begin(g, h)

    hidden(0)
    hidden(1)
    for cp in xs[0, 0]:
        cp.wait_recv()
    sel0 = routes(0)
    pick(0, sel0, 0, CH)
    hidden(2)
    for cp in xs[0, 1]:
        cp.wait_recv()
    pick(0, sel0, CH, CH)
    for cp in experts:
        cp.start()
    begin(0, 0)
    hidden(3)
    pass_on(0)
    for cp in xs[0, 2] + xs[0, 3]:
        cp.wait_recv()
    pick(0, sel0, HALF, HALF + EXT)
    begin(0, 1)
    pass_on(1)

    def gu(g):
        for r in (0, 3, 1, 2):
            shared[g, r].wait_recv()
        rows_in = tok[g, :, pl.ds(0, D)]
        acc_g[...] = lax.dot_general(rows_in, wg[...], NT, preferred_element_type=F32)
        acc_u[...] = lax.dot_general(rows_in, wu[...], NT, preferred_element_type=F32)
        ext = tok[g, :, pl.ds(D, EXT)].astype(F32)
        row_scale = ext[:, 0:1] + ext[:, 1:2] + ext[:, 2:3]
        gate = acc_g[...] * row_scale
        act[...] = (gate / (1.0 + jnp.exp(-gate)) * (acc_u[...] * row_scale)).astype(BF)

    def dn(g):
        for half in (1, 0):
            rs = pl.ds(half * QUAD, QUAD)
            for k in range(2):
                ks = pl.ds(k * HALF, HALF)
                part[g, rs, ks] = jnp.dot(act[rs, :], wd[:, ks], preferred_element_type=F32).astype(BF)
            if half == 1:
                passed = go(remote(part.at[g, rs], drecv.at[g], e_s.at[g], e_r.at[g], sib))
        return passed

    def add(dst, srcs, at, width):
        def step(i, carry):
            ks = pl.ds(pl.multiple_of(at + i * 512, 512), 512)
            total = dst[:, ks].astype(F32)
            for s in srcs:
                total = total + s[:, ks].astype(F32)
            dst[:, ks] = total.astype(BF)
            return carry

        lax.fori_loop(0, width // 512, step, 0)

    def prt(g, r):
        return part.at[g, pl.ds(r * BLK, BLK)]

    def back_q1(g, esend):
        esend.wait_recv()
        add(part.at[g, pl.ds(0, QUAD)], [drecv.at[g]], 0, D)
        f_lo = go(remote(prt(g, 2).at[:, LO], fq.at[g, :, LO], q_s.at[g, 0], q_r.at[g, 0], at_q(1)))
        f_hi = go(remote(prt(g, 2).at[:, HI], fq.at[g, :, HI], q_s.at[g, 1], q_r.at[g, 1], at_q(3)))
        n1 = go(remote(prt(g, 1).at[:, HI], nl.at[g, :, HI], q_s.at[g, 2], q_r.at[g, 2], at_q(1)))
        n3 = go(remote(prt(g, 3).at[:, LO], nr.at[g, :, LO], q_s.at[g, 3], q_r.at[g, 3], at_q(3)))
        return [f_lo, f_hi, n1, n3]

    def back_q2(g, st):
        st[0].wait_recv()
        add(prt(g, 1), [fq.at[g]], 0, HALF)
        n1 = go(remote(prt(g, 1).at[:, LO], nl.at[g, :, LO], q_s.at[g, 4], q_r.at[g, 4], at_q(1)))
        st[1].wait_recv()
        add(prt(g, 3), [fq.at[g]], HALF, HALF)
        n3 = go(remote(prt(g, 3).at[:, HI], nr.at[g, :, HI], q_s.at[g, 5], q_r.at[g, 5], at_q(3)))
        st += [n1, n3]

    def back_q3(g, st):
        for cp in st[2:]:
            cp.wait_recv()
        add(prt(g, 0), [nl.at[g], nr.at[g]], 0, D)

    home = {}

    def back(g, j):
        return part.at[g, pl.ds(QUAD + j * TOK, TOK)]

    def leave(g, st, passed):
        passed.wait_send()
        sent[:] = [cp for cp in sent if cp is not passed]
        for cp in st[2:]:
            cp.wait_recv()
        home[g] = []
        take = onehot[g][:, 0:64].astype(BF)
        factor = jnp.sum(selw[g], axis=1, keepdims=True)
        for k in range(2):
            for i in (2 * k, 2 * k + 1):
                ks = cols(i)
                total = prt(g, 0)[:, ks].astype(F32) + nl[g, :, ks].astype(F32) + nr[g, :, ks].astype(F32)
                part[g, pl.ds(QUAD, 4 * TOK), ks] = lax.dot_general(
                    take, (total * factor).astype(BF), (((0,), (0,)), ((), ())), preferred_element_type=F32
                ).astype(BF)
            ks = pl.ds(k * HALF, HALF)
            home[g].append([
                go(remote(back(g, j).at[:, ks], xr.at[g, j - 1, :, ks], o_s.at[g, k, j - 1], o_r.at[g, k, j - 1], at_x(j)))
                for j in (1, 2, 3)
            ])

    def over_x(g, k):
        ks = pl.ds(k * HALF, HALF)
        for cp in home[g][k]:
            cp.wait_recv()
        total = part[g, pl.ds(QUAD, TOK), ks].astype(F32)
        for j in range(3):
            total = total + xr[g, j, :, ks].astype(F32)
        return total

    ends = {}

    def onward(g):
        for k in range(2):
            ks = pl.ds(k * HALF, HALF)
            part[g, pl.ds(QUAD, TOK), ks] = over_x(g, k).astype(BF)
            ends[g, k] = go(remote(back(g, 0).at[:, ks], yr.at[3 - g, :, ks], p_s.at[g - 1, k], p_r.at[g - 1, k], at_p(g)))

    relay_q(0)
    enter(3)
    far_q(0)
    for cp in experts:
        cp.wait()
    enter(1)
    relay_q(3)
    gu(0)
    e0 = dn(0)
    enter(2)
    relay_q(1)
    far_q(3)
    gu(3)
    r0 = back_q1(0, e0)
    relay_q(2)
    e3 = dn(3)
    far_q(1)
    gu(1)
    back_q2(0, r0)
    e1 = dn(1)
    r3 = back_q1(3, e3)
    far_q(2)
    leave(0, r0, e0)
    gu(2)
    back_q2(3, r3)
    e2 = dn(2)
    r1 = back_q1(1, e1)
    leave(3, r3, e3)
    r2 = back_q1(2, e2)
    back_q2(1, r1)
    onward(3)
    back_q2(2, r2)
    leave(1, r1, e1)
    leave(2, r2, e2)
    onward(1)
    onward(2)
    for k in range(2):
        ks = pl.ds(k * HALF, HALF)
        total = hid[:, ks] + over_x(0, k)
        for g in (3, 1, 2):
            ends[g, k].wait_recv()
            total = total + yr[3 - g, :, ks].astype(F32)
        out[:, ks] = total.astype(BF)
    for cp in sent:
        cp.wait_send()


def body(attn_heads, residual, out_weight, norm_gain, route_ids, route_weights, gate_weights, up_weights, down_weights):
    vmem = pl.BlockSpec(memory_space=pltpu.VMEM)
    hbm = pl.BlockSpec(memory_space=pl.ANY)
    dma = pltpu.SemaphoreType.DMA
    V = pltpu.VMEM
    return pl.pallas_call(
        kernel,
        out_shape=jax.ShapeDtypeStruct((TOK, D), BF),
        in_specs=[vmem, vmem, hbm, vmem, vmem, vmem, hbm, hbm, hbm],
        out_specs=vmem,
        scratch_shapes=[
            V((512, D), BF), V((FF, D), BF), V((FF, D), BF), V((FF, D), BF),
            V((4, 2, TOK, D), BF), V((4, TOK, D), BF), V((3, TOK, D), BF),
            V((TOK, D), F32), V((128, 128), F32), V((4, BLK, 128), F32), V((4, BLK, 128), F32), V((4, 4 * TOK, WID), BF),
            V((4, GRP, D + EXT), BF), V((4, GRP, D), BF), V((4, QUAD, D), BF),
            V((4, BLK, D), BF), V((4, BLK, D), BF), V((4, BLK, D), BF),
            V((GRP, FF), F32), V((GRP, FF), F32), V((GRP, FF), BF),
            V((4, 3, TOK, D), BF), V((3, TOK, D), BF),
            dma((NCH + 3,)),
            dma((NCH,)), dma((NCH,)), dma((NCH, 3)), dma((NCH, 3)),
            dma((4, NCH, 3)), dma((4, NCH, 3)), dma((NCH, 3)), dma((NCH, 3)), dma((4, 6)), dma((4, 6)),
            dma((4, 4)), dma((4, 4)), dma((4,)), dma((4,)),
            dma((4, 6)), dma((4, 6)), dma((3, 2)), dma((3, 2)),
            dma((4, 2, 3)), dma((4, 2, 3)),
        ],
        compiler_params=pltpu.CompilerParams(
            collective_id=0, has_side_effects=True, vmem_limit_bytes=60 * 2**20
        ),
    )(attn_heads, residual, out_weight, norm_gain.reshape(1, D), route_ids.T, route_weights.T, gate_weights, up_weights, down_weights)


def solution(mesh):
    placed = (
        P("dp", "mp"),
        P(("dp", "mp"), None),
        P("mp", None),
        P(),
        P(("dp", "mp"), None),
        P(("dp", "mp"), None),
        P("dp", "mp", None),
        P("dp", "mp", None),
        P("dp", "mp", None),
    )
    return jax.shard_map(
        body, mesh=mesh, in_specs=placed, out_specs=P(("dp", "mp"), None), check_vma=False
    )
```

```python
import jax
import jax.numpy as jnp
from jax import lax
from jax.experimental import pallas as pl
from jax.experimental.pallas import tpu as pltpu
from jax.sharding import PartitionSpec as P

MESH = pl.DeviceIdType.MESH
BF = jnp.bfloat16
F32 = jnp.float32
D = 4096
CAP = 12
TOK = 16
FF = 448
BLK = 48
QUAD = 4 * BLK
GRP = 2 * QUAD
HALF = D // 2
NCH = 4
CH = D // NCH
EXT = 128
WID = EXT + D + EXT
LO = pl.ds(0, HALF)
HI = pl.ds(HALF, HALF)
HX = pl.ds(HALF, HALF + EXT)
NT = (((1,), (1,)), ((), ()))


def mod4(v):
    return lax.rem(v, 4)


def kernel(
    attn, resid, ow_h, gain, ids, rw, g_h, u_h, d_h, out,
    ow, wg, wu, wd, pbuf, sibp, zr, hid, turn, selw, onehot, nb,
    tok, part, drecv, fq, nl, nr, acc_g, acc_u, act, xr, yr,
    wsem, ps_s, ps_r, z_s, z_r, x_s, x_r, a_s, a_r, b_s, b_r,
    d_s, d_r, e_s, e_r, q_s, q_r, p_s, p_r, o_s, o_r,
):
    dp = lax.axis_index("dp")
    mp = lax.axis_index("mp")
    x, y = lax.div(dp, 4), lax.rem(dp, 4)
    z, c = lax.div(mp, 2), lax.rem(mp, 2)
    o = 1 - c
    p = y * o + z * c
    q = z * o + y * c

    def at_p(k):
        t = mod4(p + k)
        return (x * 4 + t * o + q * c, (q * o + t * c) * 2 + c)

    def at_q(k):
        t = mod4(q + k)
        return (x * 4 + p * o + t * c, (t * o + p * c) * 2 + c)

    def at_x(k):
        return (mod4(x + k) * 4 + y, mp)

    def at_z(k):
        return (dp, mod4(z + k) * 2 + c)

    def at_y(k):
        return (x * 4 + mod4(y + k), mp)

    sib = (dp, z * 2 + o)
    sent = []

    def remote(src, dst, ss, rs, dev):
        return pltpu.make_async_remote_copy(
            src_ref=src, dst_ref=dst, send_sem=ss, recv_sem=rs, device_id=dev, device_id_type=MESH
        )

    def go(copy):
        copy.start()
        sent.append(copy)
        return copy

    def cols(k):
        return pl.ds(k * CH, CH)

    loads = [pltpu.make_async_copy(ow_h.at[:, cols(k)], ow.at[:, cols(k)], wsem.at[k]) for k in range(NCH)]
    experts = [
        pltpu.make_async_copy(g_h.at[0], wg, wsem.at[NCH]),
        pltpu.make_async_copy(u_h.at[0], wu, wsem.at[NCH + 1]),
        pltpu.make_async_copy(d_h.at[0], wd, wsem.at[NCH + 2]),
    ]
    for cp in loads:
        cp.start()

    def terms(v):
        first = v.astype(BF).astype(F32)
        second = (v - first).astype(BF).astype(F32)
        return first, second, v - first - second

    turn[...] = jnp.zeros((128, 128), F32)
    turn[0:2, 0:TOK] = ids[...].astype(F32)
    for n, v in enumerate(terms(rw[...])):
        turn[2 + 2 * n : 4 + 2 * n, 0:TOK] = v
    nb[0, pl.ds(0, TOK), pl.ds(0, EXT)] = turn[...].T[0:TOK].astype(BF)
    turn[...] = jnp.zeros((128, 128), F32)

    barrier = pltpu.get_barrier_semaphore()
    greet = [sib, at_x(1), at_x(2), at_x(3), at_z(1), at_z(2), at_z(3), at_y(1), at_y(2), at_y(3)]
    for dev in greet:
        pl.semaphore_signal(barrier, inc=1, device_id=dev, device_id_type=MESH)
    for k in range(NCH):
        loads[k].wait()
        pr = jnp.dot(attn[...], ow[:, cols(k)], preferred_element_type=F32)
        pbuf[:, :, :, cols(k)] = pr.astype(BF).reshape(4, 2, TOK, CH)
    pl.semaphore_wait(barrier, len(greet))

    sibs = [
        go(remote(pbuf.at[:, o, :, cols(k)], sibp.at[:, :, cols(k)], ps_s.at[k], ps_r.at[k], sib)) for k in range(NCH)
    ]
    zs = []
    for k in range(NCH):
        sibs[k].wait_recv()
        sibp[:, :, cols(k)] = (pbuf[:, c, :, cols(k)].astype(F32) + sibp[:, :, cols(k)].astype(F32)).astype(BF)
        zs.append([
            go(remote(sibp.at[mod4(z + j), :, cols(k)], zr.at[j - 1, :, cols(k)], z_s.at[k, j - 1], z_r.at[k, j - 1], at_z(j)))
            for j in (1, 2, 3)
        ])
    def at(k):
        return pl.ds(k * CH + (EXT if k else 0), CH + (EXT if k in (0, NCH - 1) else 0))

    def body_of(k):
        return pl.ds(EXT + k * CH, CH)

    square, xs, ps = [], {}, {}

    def along_x(g, k, span):
        xs[g, k] = [
            go(remote(nb.at[g, pl.ds(0, TOK), span], nb.at[g, pl.ds((4 - j) * TOK, TOK), span], x_s.at[g, k, j - 1], x_r.at[g, k, j - 1], at_x(j)))
            for j in (1, 2, 3)
        ]

    def along_p(k):
        ps[k] = [
            go(remote(nb.at[0, pl.ds(0, TOK), at(k)], nb.at[4 - j, pl.ds(0, TOK), at(k)], a_s.at[k, j - 1], a_r.at[k, j - 1], at_p(j)))
            for j in (1, 2, 3)
        ]

    def hidden(k):
        for cp in zs[k]:
            cp.wait_recv()
        h = resid[:, cols(k)].astype(F32) + sibp[z, :, cols(k)].astype(F32)
        for j in range(3):
            h = h + zr[j, :, cols(k)].astype(F32)
        hid[:, cols(k)] = h
        square.append(jnp.sum(h * h, axis=1, keepdims=True))
        nb[0, pl.ds(0, TOK), body_of(k)] = (h * gain[:, cols(k)]).astype(BF)
        if k == NCH - 1:
            first, second, third = terms(lax.rsqrt((square[0] + square[1] + square[2] + square[3]) * (1.0 / D) + 1e-05))
            lane = lax.broadcasted_iota(jnp.int32, (TOK, EXT), 1)
            nb[0, pl.ds(0, TOK), pl.ds(EXT + D, EXT)] = jnp.where(
                lane == 0, first, jnp.where(lane == 1, second, jnp.where(lane == 2, third, 0.0))
            ).astype(BF)
        along_x(0, k, at(k))
        along_p(k)

    xf = x.astype(F32)

    def routes(g):
        turn[0 : 4 * TOK, :] = nb[g, :, pl.ds(0, EXT)].astype(F32)
        tr = turn[...].T
        col = lax.broadcasted_iota(jnp.int32, (8, 128), 1)
        in0 = jnp.logical_and(tr[0:1, :] == xf, col[0:1] < 64)
        in1 = jnp.logical_and(tr[1:2, :] == xf, col[0:1] < 64)
        uses = jnp.where(jnp.logical_or(in0, in1), 1.0, 0.0).astype(F32)
        w0 = tr[2:3, :] + tr[4:5, :] + tr[6:7, :]
        w1 = tr[3:4, :] + tr[5:6, :] + tr[7:8, :]
        weight = jnp.where(in0, w0, 0.0) + jnp.where(in1, w1, 0.0)
        ra = lax.broadcasted_iota(jnp.int32, (128, 128), 0)
        rb = lax.broadcasted_iota(jnp.int32, (128, 128), 1)
        earlier = jnp.where(jnp.logical_and(lax.div(ra, TOK) == lax.div(rb, TOK), ra < rb), 1.0, 0.0).astype(F32)
        rank = jnp.dot(jnp.broadcast_to(uses, (8, 128)), earlier, preferred_element_type=F32)
        slot = rank + (lax.div(col, TOK) * CAP).astype(F32)
        rows = lax.broadcasted_iota(jnp.int32, (BLK, 128), 0).astype(F32)
        hit = jnp.logical_and(rows == slot[0:1, :], uses > 0.5)
        selw[g] = jnp.where(hit, weight, 0.0)
        onehot[g] = jnp.where(hit, 1.0, 0.0)
        return jnp.where(hit, 1.0, 0.0).astype(BF)[:, 0:64]

    def pick(g, sel, start, width):
        tok[g, pl.ds(0, BLK), pl.ds(start, width)] = jnp.dot(
            sel, nb[g, :, pl.ds(EXT + start, width)], preferred_element_type=F32
        ).astype(BF)

    def blk(g, color, r):
        return tok.at[g, pl.ds(color * QUAD + r * BLK, BLK)]

    HV = (LO, HX)
    NV = (pl.ds(0, EXT + HALF), pl.ds(EXT + HALF, HALF + EXT))

    def near_q(g, h):
        s = blk(g, 0, 0).at[:, HV[h]]
        return [
            go(remote(s, blk(g, 0, 3).at[:, HV[h]], b_s.at[g, h], b_r.at[g, h], at_q(1))),
            go(remote(s, blk(g, 0, 1).at[:, HV[h]], b_s.at[g, 2 + h], b_r.at[g, 2 + h], at_q(3))),
        ]

    def share(g, r):
        return go(remote(blk(g, 0, r), blk(g, 1, r), d_s.at[g, r], d_r.at[g, r], sib))

    qn, shared, qf = [[None, None] for _ in range(4)], {}, [None] * 4

    def relay_q(g):
        qn[g][0][0].wait_recv()
        lo = go(remote(blk(g, 0, 3).at[:, LO], blk(g, 0, 2).at[:, LO], b_s.at[g, 4], b_r.at[g, 4], at_q(1)))
        qn[g][1][1].wait_recv()
        hi = go(remote(blk(g, 0, 1).at[:, HX], blk(g, 0, 2).at[:, HX], b_s.at[g, 5], b_r.at[g, 5], at_q(3)))
        qf[g] = (lo, hi)
        qn[g][1][0].wait_recv()
        shared[g, 3] = share(g, 3)
        qn[g][0][1].wait_recv()
        shared[g, 1] = share(g, 1)

    def far_q(g):
        qf[g][0].wait_recv()
        qf[g][1].wait_recv()
        shared[g, 2] = share(g, 2)

    def begin(g, h):
        qn[g][h] = near_q(g, h)
        if h == 1:
            shared[g, 0] = share(g, 0)

    def pass_on(h):
        for g in (3, 1, 2):
            for k in (2 * h, 2 * h + 1):
                ps[k][3 - g].wait_recv()
            along_x(g, h, NV[h])

    def enter(g):
        for h in range(2):
            for cp in xs[g, h]:
                cp.wait_recv()
            if h == 0:
                sel = routes(g)
                pick(g, sel, 0, HALF)
            else:
                pick(g, sel, HALF, HALF + EXT)
            begin(g, h)

    hidden(0)
    hidden(1)
    for cp in xs[0, 0]:
        cp.wait_recv()
    sel0 = routes(0)
    pick(0, sel0, 0, CH)
    hidden(2)
    for cp in xs[0, 1]:
        cp.wait_recv()
    pick(0, sel0, CH, CH)
    for cp in experts:
        cp.start()
    begin(0, 0)
    hidden(3)
    pass_on(0)
    for cp in xs[0, 2] + xs[0, 3]:
        cp.wait_recv()
    pick(0, sel0, HALF, HALF + EXT)
    begin(0, 1)
    pass_on(1)

    def gu(g):
        for r in (0, 3, 1, 2):
            shared[g, r].wait_recv()
        rows_in = tok[g, :, pl.ds(0, D)]
        acc_g[...] = lax.dot_general(rows_in, wg[...], NT, preferred_element_type=F32)
        acc_u[...] = lax.dot_general(rows_in, wu[...], NT, preferred_element_type=F32)
        ext = tok[g, :, pl.ds(D, EXT)].astype(F32)
        row_scale = ext[:, 0:1] + ext[:, 1:2] + ext[:, 2:3]
        gate = acc_g[...] * row_scale
        act[...] = (gate / (1.0 + jnp.exp(-gate)) * (acc_u[...] * row_scale)).astype(BF)

    def dn(g):
        for half in (1, 0):
            rs = pl.ds(half * QUAD, QUAD)
            for k in range(2):
                ks = pl.ds(k * HALF, HALF)
                part[g, rs, ks] = jnp.dot(act[rs, :], wd[:, ks], preferred_element_type=F32).astype(BF)
            if half == 1:
                passed = go(remote(part.at[g, rs], drecv.at[g], e_s.at[g], e_r.at[g], sib))
        return passed

    def add(dst, srcs, at, width):
        def step(i, carry):
            ks = pl.ds(pl.multiple_of(at + i * 512, 512), 512)
            total = dst[:, ks].astype(F32)
            for s in srcs:
                total = total + s[:, ks].astype(F32)
            dst[:, ks] = total.astype(BF)
            return carry

        lax.fori_loop(0, width // 512, step, 0)

    def prt(g, r):
        return part.at[g, pl.ds(r * BLK, BLK)]

    def back_q1(g, esend):
        esend.wait_recv()
        add(part.at[g, pl.ds(0, QUAD)], [drecv.at[g]], 0, D)
        f_lo = go(remote(prt(g, 2).at[:, LO], fq.at[g, :, LO], q_s.at[g, 0], q_r.at[g, 0], at_q(1)))
        f_hi = go(remote(prt(g, 2).at[:, HI], fq.at[g, :, HI], q_s.at[g, 1], q_r.at[g, 1], at_q(3)))
        n1 = go(remote(prt(g, 1).at[:, HI], nl.at[g, :, HI], q_s.at[g, 2], q_r.at[g, 2], at_q(1)))
        n3 = go(remote(prt(g, 3).at[:, LO], nr.at[g, :, LO], q_s.at[g, 3], q_r.at[g, 3], at_q(3)))
        return [f_lo, f_hi, n1, n3]

    def back_q2(g, st):
        st[0].wait_recv()
        add(prt(g, 1), [fq.at[g]], 0, HALF)
        n1 = go(remote(prt(g, 1).at[:, LO], nl.at[g, :, LO], q_s.at[g, 4], q_r.at[g, 4], at_q(1)))
        st[1].wait_recv()
        add(prt(g, 3), [fq.at[g]], HALF, HALF)
        n3 = go(remote(prt(g, 3).at[:, HI], nr.at[g, :, HI], q_s.at[g, 5], q_r.at[g, 5], at_q(3)))
        st += [n1, n3]

    def back_q3(g, st):
        for cp in st[2:]:
            cp.wait_recv()
        add(prt(g, 0), [nl.at[g], nr.at[g]], 0, D)

    home = {}

    def back(g, j):
        return part.at[g, pl.ds(QUAD + j * TOK, TOK)]

    def leave(g, st, passed):
        passed.wait_send()
        sent[:] = [cp for cp in sent if cp is not passed]
        for cp in st[2:]:
            cp.wait_recv()
        home[g] = []
        take = onehot[g][:, 0:64].astype(BF)
        factor = jnp.sum(selw[g], axis=1, keepdims=True)
        for k in range(2):
            for i in (2 * k, 2 * k + 1):
                ks = cols(i)
                total = prt(g, 0)[:, ks].astype(F32) + nl[g, :, ks].astype(F32) + nr[g, :, ks].astype(F32)
                part[g, pl.ds(QUAD, 4 * TOK), ks] = lax.dot_general(
                    take, (total * factor).astype(BF), (((0,), (0,)), ((), ())), preferred_element_type=F32
                ).astype(BF)
            ks = pl.ds(k * HALF, HALF)
            home[g].append([
                go(remote(back(g, j).at[:, ks], xr.at[g, j - 1, :, ks], o_s.at[g, k, j - 1], o_r.at[g, k, j - 1], at_x(j)))
                for j in (1, 2, 3)
            ])

    def over_x(g, k):
        ks = pl.ds(k * HALF, HALF)
        for cp in home[g][k]:
            cp.wait_recv()
        total = part[g, pl.ds(QUAD, TOK), ks].astype(F32)
        for j in range(3):
            total = total + xr[g, j, :, ks].astype(F32)
        return total

    ends = {}

    def onward(g):
        for k in range(2):
            ks = pl.ds(k * HALF, HALF)
            part[g, pl.ds(QUAD, TOK), ks] = over_x(g, k).astype(BF)
            ends[g, k] = go(remote(back(g, 0).at[:, ks], yr.at[3 - g, :, ks], p_s.at[g - 1, k], p_r.at[g - 1, k], at_p(g)))

    relay_q(0)
    enter(3)
    far_q(0)
    for cp in experts:
        cp.wait()
    enter(1)
    relay_q(3)
    gu(0)
    e0 = dn(0)
    enter(2)
    relay_q(1)
    far_q(3)
    gu(3)
    r0 = back_q1(0, e0)
    relay_q(2)
    e3 = dn(3)
    far_q(1)
    gu(1)
    back_q2(0, r0)
    e1 = dn(1)
    r3 = back_q1(3, e3)
    far_q(2)
    leave(0, r0, e0)
    gu(2)
    back_q2(3, r3)
    e2 = dn(2)
    r1 = back_q1(1, e1)
    leave(3, r3, e3)
    r2 = back_q1(2, e2)
    back_q2(1, r1)
    back_q2(2, r2)
    leave(1, r1, e1)
    onward(3)
    leave(2, r2, e2)
    onward(1)
    onward(2)
    for k in range(2):
        ks = pl.ds(k * HALF, HALF)
        total = hid[:, ks] + over_x(0, k)
        for g in (3, 1, 2):
            ends[g, k].wait_recv()
            total = total + yr[3 - g, :, ks].astype(F32)
        out[:, ks] = total.astype(BF)
    for cp in sent:
        cp.wait_send()


def body(attn_heads, residual, out_weight, norm_gain, route_ids, route_weights, gate_weights, up_weights, down_weights):
    vmem = pl.BlockSpec(memory_space=pltpu.VMEM)
    hbm = pl.BlockSpec(memory_space=pl.ANY)
    dma = pltpu.SemaphoreType.DMA
    V = pltpu.VMEM
    return pl.pallas_call(
        kernel,
        out_shape=jax.ShapeDtypeStruct((TOK, D), BF),
        in_specs=[vmem, vmem, hbm, vmem, vmem, vmem, hbm, hbm, hbm],
        out_specs=vmem,
        scratch_shapes=[
            V((512, D), BF), V((FF, D), BF), V((FF, D), BF), V((FF, D), BF),
            V((4, 2, TOK, D), BF), V((4, TOK, D), BF), V((3, TOK, D), BF),
            V((TOK, D), F32), V((128, 128), F32), V((4, BLK, 128), F32), V((4, BLK, 128), F32), V((4, 4 * TOK, WID), BF),
            V((4, GRP, D + EXT), BF), V((4, GRP, D), BF), V((4, QUAD, D), BF),
            V((4, BLK, D), BF), V((4, BLK, D), BF), V((4, BLK, D), BF),
            V((GRP, FF), F32), V((GRP, FF), F32), V((GRP, FF), BF),
            V((4, 3, TOK, D), BF), V((3, TOK, D), BF),
            dma((NCH + 3,)),
            dma((NCH,)), dma((NCH,)), dma((NCH, 3)), dma((NCH, 3)),
            dma((4, NCH, 3)), dma((4, NCH, 3)), dma((NCH, 3)), dma((NCH, 3)), dma((4, 6)), dma((4, 6)),
            dma((4, 4)), dma((4, 4)), dma((4,)), dma((4,)),
            dma((4, 6)), dma((4, 6)), dma((3, 2)), dma((3, 2)),
            dma((4, 2, 3)), dma((4, 2, 3)),
        ],
        compiler_params=pltpu.CompilerParams(
            collective_id=0, has_side_effects=True, vmem_limit_bytes=60 * 2**20
        ),
    )(attn_heads, residual, out_weight, norm_gain.reshape(1, D), route_ids.T, route_weights.T, gate_weights, up_weights, down_weights)


def solution(mesh):
    placed = (
        P("dp", "mp"),
        P(("dp", "mp"), None),
        P("mp", None),
        P(),
        P(("dp", "mp"), None),
        P(("dp", "mp"), None),
        P("dp", "mp", None),
        P("dp", "mp", None),
        P("dp", "mp", None),
    )
    return jax.shard_map(
        body, mesh=mesh, in_specs=placed, out_specs=P(("dp", "mp"), None), check_vma=False
    )
```

```python
import jax
import jax.numpy as jnp
from jax import lax
from jax.experimental import pallas as pl
from jax.experimental.pallas import tpu as pltpu
from jax.sharding import PartitionSpec as P

MESH = pl.DeviceIdType.MESH
BF = jnp.bfloat16
F32 = jnp.float32
D = 4096
CAP = 12
TOK = 16
FF = 448
BLK = 48
QUAD = 4 * BLK
GRP = 2 * QUAD
HALF = D // 2
NCH = 4
CH = D // NCH
EXT = 128
WID = EXT + D + EXT
LO = pl.ds(0, HALF)
HI = pl.ds(HALF, HALF)
HX = pl.ds(HALF, HALF + EXT)
NT = (((1,), (1,)), ((), ()))


def mod4(v):
    return lax.rem(v, 4)


def kernel(
    attn, resid, ow_h, gain, ids, rw, g_h, u_h, d_h, out,
    ow, wg, wu, wd, pbuf, sibp, zr, hid, turn, selw, onehot, nb,
    tok, part, drecv, fq, nl, nr, acc_g, acc_u, act, xr, yr,
    wsem, ps_s, ps_r, z_s, z_r, x_s, x_r, a_s, a_r, b_s, b_r,
    d_s, d_r, e_s, e_r, q_s, q_r, p_s, p_r, o_s, o_r,
):
    dp = lax.axis_index("dp")
    mp = lax.axis_index("mp")
    x, y = lax.div(dp, 4), lax.rem(dp, 4)
    z, c = lax.div(mp, 2), lax.rem(mp, 2)
    o = 1 - c
    p = y * o + z * c
    q = z * o + y * c

    def at_p(k):
        t = mod4(p + k)
        return (x * 4 + t * o + q * c, (q * o + t * c) * 2 + c)

    def at_q(k):
        t = mod4(q + k)
        return (x * 4 + p * o + t * c, (t * o + p * c) * 2 + c)

    def at_x(k):
        return (mod4(x + k) * 4 + y, mp)

    def at_z(k):
        return (dp, mod4(z + k) * 2 + c)

    def at_y(k):
        return (x * 4 + mod4(y + k), mp)

    sib = (dp, z * 2 + o)
    sent = []

    def remote(src, dst, ss, rs, dev):
        return pltpu.make_async_remote_copy(
            src_ref=src, dst_ref=dst, send_sem=ss, recv_sem=rs, device_id=dev, device_id_type=MESH
        )

    def go(copy):
        copy.start()
        sent.append(copy)
        return copy

    def cols(k):
        return pl.ds(k * CH, CH)

    loads = [pltpu.make_async_copy(ow_h.at[:, cols(k)], ow.at[:, cols(k)], wsem.at[k]) for k in range(NCH)]
    experts = [
        pltpu.make_async_copy(g_h.at[0], wg, wsem.at[NCH]),
        pltpu.make_async_copy(u_h.at[0], wu, wsem.at[NCH + 1]),
        pltpu.make_async_copy(d_h.at[0], wd, wsem.at[NCH + 2]),
    ]
    for cp in loads:
        cp.start()

    def terms(v):
        first = v.astype(BF).astype(F32)
        second = (v - first).astype(BF).astype(F32)
        return first, second, v - first - second

    turn[...] = jnp.zeros((128, 128), F32)
    turn[0:2, 0:TOK] = ids[...].astype(F32)
    for n, v in enumerate(terms(rw[...])):
        turn[2 + 2 * n : 4 + 2 * n, 0:TOK] = v
    nb[0, pl.ds(0, TOK), pl.ds(0, EXT)] = turn[...].T[0:TOK].astype(BF)
    turn[...] = jnp.zeros((128, 128), F32)

    barrier = pltpu.get_barrier_semaphore()
    greet = [sib, at_x(1), at_x(2), at_x(3), at_z(1), at_z(2), at_z(3), at_y(1), at_y(2), at_y(3)]
    for dev in greet:
        pl.semaphore_signal(barrier, inc=1, device_id=dev, device_id_type=MESH)
    for k in range(NCH):
        loads[k].wait()
        pr = jnp.dot(attn[...], ow[:, cols(k)], preferred_element_type=F32)
        pbuf[:, :, :, cols(k)] = pr.astype(BF).reshape(4, 2, TOK, CH)
    pl.semaphore_wait(barrier, len(greet))

    sibs = [
        go(remote(pbuf.at[:, o, :, cols(k)], sibp.at[:, :, cols(k)], ps_s.at[k], ps_r.at[k], sib)) for k in range(NCH)
    ]
    zs = []
    for k in range(NCH):
        sibs[k].wait_recv()
        sibp[:, :, cols(k)] = (pbuf[:, c, :, cols(k)].astype(F32) + sibp[:, :, cols(k)].astype(F32)).astype(BF)
        zs.append([
            go(remote(sibp.at[mod4(z + j), :, cols(k)], zr.at[j - 1, :, cols(k)], z_s.at[k, j - 1], z_r.at[k, j - 1], at_z(j)))
            for j in (1, 2, 3)
        ])
    def at(k):
        return pl.ds(k * CH + (EXT if k else 0), CH + (EXT if k in (0, NCH - 1) else 0))

    def body_of(k):
        return pl.ds(EXT + k * CH, CH)

    square, xs, ps = [], {}, {}

    def along_x(g, k, span):
        xs[g, k] = [
            go(remote(nb.at[g, pl.ds(0, TOK), span], nb.at[g, pl.ds((4 - j) * TOK, TOK), span], x_s.at[g, k, j - 1], x_r.at[g, k, j - 1], at_x(j)))
            for j in (1, 2, 3)
        ]

    def along_p(k):
        ps[k] = [
            go(remote(nb.at[0, pl.ds(0, TOK), at(k)], nb.at[4 - j, pl.ds(0, TOK), at(k)], a_s.at[k, j - 1], a_r.at[k, j - 1], at_p(j)))
            for j in (1, 2, 3)
        ]

    def hidden(k):
        for cp in zs[k]:
            cp.wait_recv()
        h = resid[:, cols(k)].astype(F32) + sibp[z, :, cols(k)].astype(F32)
        for j in range(3):
            h = h + zr[j, :, cols(k)].astype(F32)
        hid[:, cols(k)] = h
        square.append(jnp.sum(h * h, axis=1, keepdims=True))
        nb[0, pl.ds(0, TOK), body_of(k)] = (h * gain[:, cols(k)]).astype(BF)
        if k == NCH - 1:
            first, second, third = terms(lax.rsqrt((square[0] + square[1] + square[2] + square[3]) * (1.0 / D) + 1e-05))
            lane = lax.broadcasted_iota(jnp.int32, (TOK, EXT), 1)
            nb[0, pl.ds(0, TOK), pl.ds(EXT + D, EXT)] = jnp.where(
                lane == 0, first, jnp.where(lane == 1, second, jnp.where(lane == 2, third, 0.0))
            ).astype(BF)
        along_x(0, k, at(k))
        along_p(k)

    xf = x.astype(F32)

    def routes(g):
        turn[0 : 4 * TOK, :] = nb[g, :, pl.ds(0, EXT)].astype(F32)
        tr = turn[...].T
        col = lax.broadcasted_iota(jnp.int32, (8, 128), 1)
        in0 = jnp.logical_and(tr[0:1, :] == xf, col[0:1] < 64)
        in1 = jnp.logical_and(tr[1:2, :] == xf, col[0:1] < 64)
        uses = jnp.where(jnp.logical_or(in0, in1), 1.0, 0.0).astype(F32)
        w0 = tr[2:3, :] + tr[4:5, :] + tr[6:7, :]
        w1 = tr[3:4, :] + tr[5:6, :] + tr[7:8, :]
        weight = jnp.where(in0, w0, 0.0) + jnp.where(in1, w1, 0.0)
        ra = lax.broadcasted_iota(jnp.int32, (128, 128), 0)
        rb = lax.broadcasted_iota(jnp.int32, (128, 128), 1)
        earlier = jnp.where(jnp.logical_and(lax.div(ra, TOK) == lax.div(rb, TOK), ra < rb), 1.0, 0.0).astype(F32)
        rank = jnp.dot(jnp.broadcast_to(uses, (8, 128)), earlier, preferred_element_type=F32)
        slot = rank + (lax.div(col, TOK) * CAP).astype(F32)
        rows = lax.broadcasted_iota(jnp.int32, (BLK, 128), 0).astype(F32)
        hit = jnp.logical_and(rows == slot[0:1, :], uses > 0.5)
        selw[g] = jnp.where(hit, weight, 0.0)
        onehot[g] = jnp.where(hit, 1.0, 0.0)
        return jnp.where(hit, 1.0, 0.0).astype(BF)[:, 0:64]

    def pick(g, sel, start, width):
        tok[g, pl.ds(0, BLK), pl.ds(start, width)] = jnp.dot(
            sel, nb[g, :, pl.ds(EXT + start, width)], preferred_element_type=F32
        ).astype(BF)

    def blk(g, color, r):
        return tok.at[g, pl.ds(color * QUAD + r * BLK, BLK)]

    HV = (LO, HX)
    NV = (pl.ds(0, EXT + HALF), pl.ds(EXT + HALF, HALF + EXT))

    def near_q(g, h):
        s = blk(g, 0, 0).at[:, HV[h]]
        return [
            go(remote(s, blk(g, 0, 3).at[:, HV[h]], b_s.at[g, h], b_r.at[g, h], at_q(1))),
            go(remote(s, blk(g, 0, 1).at[:, HV[h]], b_s.at[g, 2 + h], b_r.at[g, 2 + h], at_q(3))),
        ]

    def share(g, r):
        return go(remote(blk(g, 0, r), blk(g, 1, r), d_s.at[g, r], d_r.at[g, r], sib))

    qn, shared, qf = [[None, None] for _ in range(4)], {}, [None] * 4

    def relay_q(g):
        qn[g][0][0].wait_recv()
        lo = go(remote(blk(g, 0, 3).at[:, LO], blk(g, 0, 2).at[:, LO], b_s.at[g, 4], b_r.at[g, 4], at_q(1)))
        qn[g][1][1].wait_recv()
        hi = go(remote(blk(g, 0, 1).at[:, HX], blk(g, 0, 2).at[:, HX], b_s.at[g, 5], b_r.at[g, 5], at_q(3)))
        qf[g] = (lo, hi)
        qn[g][1][0].wait_recv()
        shared[g, 3] = share(g, 3)
        qn[g][0][1].wait_recv()
        shared[g, 1] = share(g, 1)

    def far_q(g):
        qf[g][0].wait_recv()
        qf[g][1].wait_recv()
        shared[g, 2] = share(g, 2)

    def begin(g, h):
        qn[g][h] = near_q(g, h)
        if h == 1:
            shared[g, 0] = share(g, 0)

    def pass_on(h):
        for g in (3, 1, 2):
            for k in (2 * h, 2 * h + 1):
                ps[k][3 - g].wait_recv()
            along_x(g, h, NV[h])

    def enter(g):
        for h in range(2):
            for cp in xs[g, h]:
                cp.wait_recv()
            if h == 0:
                sel = routes(g)
                pick(g, sel, 0, HALF)
            else:
                pick(g, sel, HALF, HALF + EXT)
            begin(g, h)

    hidden(0)
    hidden(1)
    for cp in xs[0, 0]:
        cp.wait_recv()
    sel0 = routes(0)
    pick(0, sel0, 0, CH)
    hidden(2)
    for cp in xs[0, 1]:
        cp.wait_recv()
    pick(0, sel0, CH, CH)
    for cp in experts:
        cp.start()
    begin(0, 0)
    hidden(3)
    pass_on(0)
    for cp in xs[0, 2] + xs[0, 3]:
        cp.wait_recv()
    pick(0, sel0, HALF, HALF + EXT)
    begin(0, 1)
    pass_on(1)

    def gu(g):
        for r in (0, 3, 1, 2):
            shared[g, r].wait_recv()
        rows_in = tok[g, :, pl.ds(0, D)]
        acc_g[...] = lax.dot_general(rows_in, wg[...], NT, preferred_element_type=F32)
        acc_u[...] = lax.dot_general(rows_in, wu[...], NT, preferred_element_type=F32)
        ext = tok[g, :, pl.ds(D, EXT)].astype(F32)
        row_scale = ext[:, 0:1] + ext[:, 1:2] + ext[:, 2:3]
        gate = acc_g[...] * row_scale
        act[...] = (gate / (1.0 + jnp.exp(-gate)) * (acc_u[...] * row_scale)).astype(BF)

    def dn(g):
        for half in (1, 0):
            rs = pl.ds(half * QUAD, QUAD)
            for k in range(2):
                ks = pl.ds(k * HALF, HALF)
                part[g, rs, ks] = jnp.dot(act[rs, :], wd[:, ks], preferred_element_type=F32).astype(BF)
            if half == 1:
                passed = go(remote(part.at[g, rs], drecv.at[g], e_s.at[g], e_r.at[g], sib))
        return passed

    def add(dst, srcs, at, width):
        def step(i, carry):
            ks = pl.ds(pl.multiple_of(at + i * 512, 512), 512)
            total = dst[:, ks].astype(F32)
            for s in srcs:
                total = total + s[:, ks].astype(F32)
            dst[:, ks] = total.astype(BF)
            return carry

        lax.fori_loop(0, width // 512, step, 0)

    def prt(g, r):
        return part.at[g, pl.ds(r * BLK, BLK)]

    def back_q1(g, esend):
        esend.wait_recv()
        add(part.at[g, pl.ds(0, QUAD)], [drecv.at[g]], 0, D)
        f_lo = go(remote(prt(g, 2).at[:, LO], fq.at[g, :, LO], q_s.at[g, 0], q_r.at[g, 0], at_q(1)))
        f_hi = go(remote(prt(g, 2).at[:, HI], fq.at[g, :, HI], q_s.at[g, 1], q_r.at[g, 1], at_q(3)))
        n1 = go(remote(prt(g, 1).at[:, HI], nl.at[g, :, HI], q_s.at[g, 2], q_r.at[g, 2], at_q(1)))
        n3 = go(remote(prt(g, 3).at[:, LO], nr.at[g, :, LO], q_s.at[g, 3], q_r.at[g, 3], at_q(3)))
        return [f_lo, f_hi, n1, n3]

    def back_q2(g, st):
        st[0].wait_recv()
        add(prt(g, 1), [fq.at[g]], 0, HALF)
        n1 = go(remote(prt(g, 1).at[:, LO], nl.at[g, :, LO], q_s.at[g, 4], q_r.at[g, 4], at_q(1)))
        st[1].wait_recv()
        add(prt(g, 3), [fq.at[g]], HALF, HALF)
        n3 = go(remote(prt(g, 3).at[:, HI], nr.at[g, :, HI], q_s.at[g, 5], q_r.at[g, 5], at_q(3)))
        st += [n1, n3]

    def back_q3(g, st):
        for cp in st[2:]:
            cp.wait_recv()
        add(prt(g, 0), [nl.at[g], nr.at[g]], 0, D)

    home = {}

    def back(g, j):
        return part.at[g, pl.ds(QUAD + j * TOK, TOK)]

    def leave(g, st, passed):
        passed.wait_send()
        sent[:] = [cp for cp in sent if cp is not passed]
        for cp in st[2:]:
            cp.wait_recv()
        home[g] = []
        take = onehot[g][:, 0:64].astype(BF)
        factor = jnp.sum(selw[g], axis=1, keepdims=True)
        for k in range(2):
            for i in (2 * k, 2 * k + 1):
                ks = cols(i)
                total = prt(g, 0)[:, ks].astype(F32) + nl[g, :, ks].astype(F32) + nr[g, :, ks].astype(F32)
                part[g, pl.ds(QUAD, 4 * TOK), ks] = lax.dot_general(
                    take, (total * factor).astype(BF), (((0,), (0,)), ((), ())), preferred_element_type=F32
                ).astype(BF)
            ks = pl.ds(k * HALF, HALF)
            home[g].append([
                go(remote(back(g, j).at[:, ks], xr.at[g, j - 1, :, ks], o_s.at[g, k, j - 1], o_r.at[g, k, j - 1], at_x(j)))
                for j in (1, 2, 3)
            ])

    def over_x(g, k):
        ks = pl.ds(k * HALF, HALF)
        for cp in home[g][k]:
            cp.wait_recv()
        total = part[g, pl.ds(QUAD, TOK), ks].astype(F32)
        for j in range(3):
            total = total + xr[g, j, :, ks].astype(F32)
        return total

    ends = {}

    def onward(g):
        for k in range(2):
            ks = pl.ds(k * HALF, HALF)
            part[g, pl.ds(QUAD, TOK), ks] = over_x(g, k).astype(BF)
            ends[g, k] = go(remote(back(g, 0).at[:, ks], yr.at[3 - g, :, ks], p_s.at[g - 1, k], p_r.at[g - 1, k], at_p(g)))

    relay_q(0)
    enter(3)
    far_q(0)
    for cp in experts:
        cp.wait()
    enter(1)
    gu(0)
    relay_q(3)
    e0 = dn(0)
    enter(2)
    relay_q(1)
    far_q(3)
    gu(3)
    r0 = back_q1(0, e0)
    relay_q(2)
    e3 = dn(3)
    far_q(1)
    gu(1)
    back_q2(0, r0)
    e1 = dn(1)
    r3 = back_q1(3, e3)
    far_q(2)
    leave(0, r0, e0)
    gu(2)
    back_q2(3, r3)
    e2 = dn(2)
    r1 = back_q1(1, e1)
    leave(3, r3, e3)
    r2 = back_q1(2, e2)
    back_q2(1, r1)
    back_q2(2, r2)
    leave(1, r1, e1)
    onward(3)
    leave(2, r2, e2)
    onward(1)
    onward(2)
    for k in range(2):
        ks = pl.ds(k * HALF, HALF)
        total = hid[:, ks] + over_x(0, k)
        for g in (3, 1, 2):
            ends[g, k].wait_recv()
            total = total + yr[3 - g, :, ks].astype(F32)
        out[:, ks] = total.astype(BF)
    for cp in sent:
        cp.wait_send()


def body(attn_heads, residual, out_weight, norm_gain, route_ids, route_weights, gate_weights, up_weights, down_weights):
    vmem = pl.BlockSpec(memory_space=pltpu.VMEM)
    hbm = pl.BlockSpec(memory_space=pl.ANY)
    dma = pltpu.SemaphoreType.DMA
    V = pltpu.VMEM
    return pl.pallas_call(
        kernel,
        out_shape=jax.ShapeDtypeStruct((TOK, D), BF),
        in_specs=[vmem, vmem, hbm, vmem, vmem, vmem, hbm, hbm, hbm],
        out_specs=vmem,
        scratch_shapes=[
            V((512, D), BF), V((FF, D), BF), V((FF, D), BF), V((FF, D), BF),
            V((4, 2, TOK, D), BF), V((4, TOK, D), BF), V((3, TOK, D), BF),
            V((TOK, D), F32), V((128, 128), F32), V((4, BLK, 128), F32), V((4, BLK, 128), F32), V((4, 4 * TOK, WID), BF),
            V((4, GRP, D + EXT), BF), V((4, GRP, D), BF), V((4, QUAD, D), BF),
            V((4, BLK, D), BF), V((4, BLK, D), BF), V((4, BLK, D), BF),
            V((GRP, FF), F32), V((GRP, FF), F32), V((GRP, FF), BF),
            V((4, 3, TOK, D), BF), V((3, TOK, D), BF),
            dma((NCH + 3,)),
            dma((NCH,)), dma((NCH,)), dma((NCH, 3)), dma((NCH, 3)),
            dma((4, NCH, 3)), dma((4, NCH, 3)), dma((NCH, 3)), dma((NCH, 3)), dma((4, 6)), dma((4, 6)),
            dma((4, 4)), dma((4, 4)), dma((4,)), dma((4,)),
            dma((4, 6)), dma((4, 6)), dma((3, 2)), dma((3, 2)),
            dma((4, 2, 3)), dma((4, 2, 3)),
        ],
        compiler_params=pltpu.CompilerParams(
            collective_id=0, has_side_effects=True, vmem_limit_bytes=60 * 2**20
        ),
    )(attn_heads, residual, out_weight, norm_gain.reshape(1, D), route_ids.T, route_weights.T, gate_weights, up_weights, down_weights)


def solution(mesh):
    placed = (
        P("dp", "mp"),
        P(("dp", "mp"), None),
        P("mp", None),
        P(),
        P(("dp", "mp"), None),
        P(("dp", "mp"), None),
        P("dp", "mp", None),
        P("dp", "mp", None),
        P("dp", "mp", None),
    )
    return jax.shard_map(
        body, mesh=mesh, in_specs=placed, out_specs=P(("dp", "mp"), None), check_vma=False
    )
```
